32 devices in a mesh: tm: 2 (over x), space: 16 (over z, y, core).
Axes of the slice: x: 2, y: 2, z: 4, core: 2. Of those that a mesh axis runs over, the one named last changes fastest.
Arguments:
- initial_states: float32 [2, 5, 16, 96, 128], P('tm', None, 'space'), may hold values from -6 to 6
- terminal_states: float32 [2, 5, 16, 96, 128], P('tm', None, 'space'), may hold values from -6 to 6
- forcing: float32 [2, 2, 5, 16, 96, 128], P(None, None, None, 'space'), may hold values from -6 to 6
- density_mean: float32 [16, 96, 128], P('space'), may hold values from 0.5 to 2
- velocity_mean: float32 [3, 16, 96, 128], P(None, 'space'), may hold values from -1 to 1
- pressure_mean: float32 [16, 96, 128], P('space'), may hold values from 0.5 to 2
- sponge: float32 [16, 96, 128], P('space'), may hold values from 0.05 to 1
Outputs:
- next_initial: float32 [2, 5, 16, 96, 128], P('tm', None, 'space')
- next_terminal: float32 [2, 5, 16, 96, 128], P('tm', None, 'space')
- response: float32 [2, 2, 5, 16, 96, 128], P(None, None, None, 'space')
- adjoint_projection: float32 [2, 2, 5, 16, 96, 128], P(None, None, None, 'space', 'tm')
The draws below stay inside these ranges and needn't reach their ends.
All inputs are finite; a program needn't handle non-finite values.
Results may differ from the reference program's by a relative error of at most 0.00002.
Values sent between devices are 32-bit elements; how exact they have to be, the bound alone decides.
A program may use at most 64 MiB of HBM per device.

```python
import math
import jax
import jax.numpy as jnp
from jax import lax

NY = 96
NZ = 128
STEPS = 1
NFREQ = 2
NX = 16
SLABS = 2
N_TM = 2


def levels(rng, shape, cuts, smallest, top_value):
    level = 1.0
    for dim, shards_of in cuts:
        heights = jax.random.uniform(jax.random.fold_in(jax.random.fold_in(rng, 6), dim), (shards_of,), jnp.float32, smallest / len(cuts), top_value / len(cuts))
        level = level * jnp.repeat(jnp.exp(heights), shape[dim] // shards_of).reshape((-1,) + (1,) * (len(shape) - 1 - dim))
    return level


def noise(key, shape, scale, most, cuts=(), kind=jnp.bfloat16):
    array = jax.random.normal(key, shape, jnp.float32) * scale
    if len(cuts) > 0:
        array = levels(key, shape, cuts, -0.22, 0.18) * array
    return jnp.clip(array, min=-most, max=most).astype(kind)


def setup_inputs(seed: int = 0) -> dict:
    splits = jax.random.split(jax.random.key(seed), 8)
    initial_states = noise(splits[0], (SLABS, 5, NX, NY, NZ), 1.0, 6.0, ((0, 2), (2, 16)), jnp.float32)
    terminal_states = noise(splits[1], (SLABS, 5, NX, NY, NZ), 1.0, 6.0, ((0, 2), (2, 16)), jnp.float32)
    forcing = noise(splits[2], (NFREQ, 2, 5, NX, NY, NZ), 1.0, 6.0, ((3, 16),), jnp.float32)
    density_mean = jnp.clip(jnp.exp(math.log(2.0) - 1.3862944 * jax.random.uniform(splits[3], (NX, NY, NZ), jnp.float32) ** levels(splits[3], (NX, NY, NZ), ((0, 16),), -0.2, 0.2)), 0.5, 2.0)
    velocity_mean = jnp.clip(jax.random.uniform(splits[4], (3, NX, NY, NZ), jnp.float32, -1.0, 1.0) * levels(splits[4], (3, NX, NY, NZ), ((1, 16),), -0.4, 0.0), -1.0, 1.0)
    pressure_mean = jnp.clip(jnp.exp(math.log(2.0) - 1.3862944 * jax.random.uniform(splits[5], (NX, NY, NZ), jnp.float32) ** levels(splits[5], (NX, NY, NZ), ((0, 16),), -0.2, 0.2)), 0.5, 2.0)
    sponge = jnp.clip(jnp.exp(math.log(1.0) - 2.9957323 * jax.random.uniform(splits[6], (NX, NY, NZ), jnp.float32) ** levels(splits[6], (NX, NY, NZ), ((0, 16),), -0.2, 0.2)), 0.05, 1.0)
    return {"initial_states": initial_states, "terminal_states": terminal_states, "forcing": forcing, "density_mean": density_mean, "velocity_mean": velocity_mean, "pressure_mean": pressure_mean, "sponge": sponge}


viscosity = 0.05
time_step = 0.25

def shifted_pair(field, axis_number):
    widths = [(0, 0)] * field.ndim
    widths[axis_number] = (1, 1)
    padded = jnp.pad(field, widths)
    length = field.shape[axis_number]
    return (lax.slice_in_dim(padded, 2, length + 2, axis=axis_number), lax.slice_in_dim(padded, 0, length, axis=axis_number))

def forward_rhs(state_padded, density, velocity, pressure, sponge):
    state = state_padded[:, 1:-1]
    grad_x = 0.5 * (state_padded[:, 2:] - state_padded[:, :-2])
    y_plus, y_minus = shifted_pair(state, 2)
    z_plus, z_minus = shifted_pair(state, 3)
    grad_y = 0.5 * (y_plus - y_minus)
    grad_z = 0.5 * (z_plus - z_minus)
    laplace = state_padded[:, 2:] + state_padded[:, :-2] + y_plus + y_minus + z_plus + z_minus - 6.0 * state
    advect = velocity[0] * grad_x + velocity[1] * grad_y + velocity[2] * grad_z
    diverge = grad_x[1] + grad_y[2] + grad_z[3]
    inverse = 1.0 / density
    rows = [-advect[0] - density * diverge, -advect[1] - inverse * grad_x[4] + viscosity * laplace[1], -advect[2] - inverse * grad_y[4] + viscosity * laplace[2], -advect[3] - inverse * grad_z[4] + viscosity * laplace[3], -advect[4] - pressure * diverge + viscosity * laplace[4]]
    return jnp.stack(rows) - sponge * state

def wave_factors(half_count, total_steps):
    cosines = []
    sines = []
    for freq_index in range(NFREQ):
        turns = (freq_index + 1) * half_count % (2 * total_steps)
        angle = 2.0 * math.pi / (2 * total_steps) * jnp.asarray(turns).astype(jnp.float32)
        cosines.append(jnp.cos(angle))
        sines.append(jnp.sin(angle))
    return (cosines, sines)

def forcing_value(coeffs, half_count, total_steps):
    cosines, sines = wave_factors(half_count, total_steps)
    value = jnp.zeros(coeffs.shape[2:], jnp.float32)
    for freq_index in range(NFREQ):
        value = value + coeffs[freq_index, 0] * cosines[freq_index] - coeffs[freq_index, 1] * sines[freq_index]
    return value

def sample_terms(state, half_count, total_steps):
    cosines, sines = wave_factors(half_count, total_steps)
    return jnp.stack([jnp.stack([state * cosines[k], -state * sines[k]]) for k in range(NFREQ)])

def rk_step(state, half_count, sign_value, operator, coeffs, total_steps):
    first = operator(state) + forcing_value(coeffs, half_count, total_steps)
    second = operator(state + 0.5 * time_step * first) + forcing_value(coeffs, half_count + sign_value, total_steps)
    third = operator(state + 0.5 * time_step * second) + forcing_value(coeffs, half_count + sign_value, total_steps)
    fourth = operator(state + time_step * third) + forcing_value(coeffs, half_count + 2 * sign_value, total_steps)
    return state + time_step / 6.0 * (first + 2.0 * second + 2.0 * third + fourth)

def reference(initial_states, terminal_states, forcing, density_mean, velocity_mean, pressure_mean, sponge):
    total_steps = N_TM * STEPS

    def operate(state):
        padded = jnp.pad(state, ((0, 0), (1, 1), (0, 0), (0, 0)))
        return forward_rhs(padded, density_mean, velocity_mean, pressure_mean, sponge)
    zero_state = jnp.zeros(initial_states.shape[1:], jnp.float32)
    unused, pullback = jax.vjp(operate, zero_state)

    def adjoint_operate(adjoint):
        return pullback(adjoint)[0]
    finals = []
    response = jnp.zeros(forcing.shape, jnp.float32)
    for slab_index in range(N_TM):
        state = initial_states[slab_index]
        for step_index in range(STEPS):
            half_count = 2 * (slab_index * STEPS + step_index)
            response = response + sample_terms(state, half_count, total_steps)
            state = rk_step(state, half_count, 1, operate, forcing, total_steps)
        finals.append(state)
    response = response / total_steps
    reaction = 2.0 * response
    starts = []
    projection = jnp.zeros(forcing.shape, jnp.float32)
    for slab_index in range(N_TM):
        adjoint = terminal_states[slab_index]
        for step_index in range(STEPS):
            half_count = 2 * (slab_index * STEPS + STEPS - step_index)
            adjoint = rk_step(adjoint, half_count, -1, adjoint_operate, reaction, total_steps)
            projection = projection + sample_terms(adjoint, half_count - 2, total_steps)
        starts.append(adjoint)
    projection = projection / total_steps
    next_initial = jnp.stack([finals[(slab - 1) % N_TM] for slab in range(N_TM)])
    next_terminal = jnp.stack([starts[(slab + 1) % N_TM] for slab in range(N_TM)])
    return (next_initial, next_terminal, response, projection)
```

```python
import functools
import math

import jax
import jax.numpy as jnp
from jax import lax
from jax.experimental import pallas as pl
from jax.experimental.pallas import tpu as pltpu
from jax.sharding import PartitionSpec as P

NFREQ = 2
viscosity = 0.05
time_step = 0.25
MESH = pl.DeviceIdType.MESH

R_INIT, R_COEF, R_TERM, R_F0, R_F1, C_SIB, C_EXT = range(7)
HALO = 7
FINAL = HALO + 24
SLAB = FINAL + 5


def theta(k, half_count, slabs):
    turns = (k + 1) * half_count % (2 * slabs)
    return 2.0 * math.pi * turns / (2 * slabs)


def picked(values, index):
    out = jnp.float32(values[0])
    for j in range(1, len(values)):
        out = jnp.where(index == j, jnp.float32(values[j]), out)
    return out


def force_factors(slab, offset, n):
    rows = []
    for k in range(NFREQ):
        rows.append(picked([math.cos(theta(k, 2 * j + offset, n)) for j in range(n)], slab))
        rows.append(picked([-math.sin(theta(k, 2 * j + offset, n)) for j in range(n)], slab))
    return rows


def react_factor(half_gap, n):
    return 2.0 / n * sum(math.cos(theta(k, half_gap, n)) for k in range(NFREQ))


def shift_y(x, above, below, rows):
    n = x.shape[0]
    minus = jnp.where(rows == 0, above, pltpu.roll(x, 1, 0))
    plus = jnp.where(rows == n - 1, below, pltpu.roll(x, n - 1, 0))
    return plus, minus


def shift_z(x, lanes):
    n = x.shape[1]
    minus = jnp.where(lanes == 0, 0.0, pltpu.roll(x, 1, 1))
    plus = jnp.where(lanes == n - 1, 0.0, pltpu.roll(x, n - 1, 1))
    return plus, minus


def forward_plane(c, lo, hi, w, halo_row, first, rows, lanes):
    rho, u1, u2, u3, pres, sponge, inv = [w(i) for i in range(7)]
    out = [None] * 5
    for f in range(5):
        v, a, b = c(f), lo(f), hi(f)
        r = halo_row(f)
        yp, ym = shift_y(v, jnp.where(first, 0.0, r), jnp.where(first, r, 0.0), rows)
        zp, zm = shift_z(v, lanes)
        dx, dy, dz = 0.5 * (b - a), 0.5 * (yp - ym), 0.5 * (zp - zm)
        o = -(u1 * dx + u2 * dy + u3 * dz) - sponge * v
        if f > 0:
            o = o + viscosity * ((a + b) + (yp + ym) + (zp + zm) - 6.0 * v)
        if f == 1:
            div = dx
        elif f == 2:
            div = div + dy
        elif f == 3:
            div = div + dz
        elif f == 4:
            out[1] = out[1] - inv * dx
            out[2] = out[2] - inv * dy
            out[3] = out[3] - inv * dz
        out[f] = o
    out[0] = out[0] - rho * div
    out[4] = out[4] - pres * div
    return out


def flux(a, rho, inv, speed, pres, direction):
    rows = [speed * a[i] for i in range(5)]
    rows[1 + direction] = rows[1 + direction] + rho * a[0] + pres * a[4]
    rows[4] = rows[4] + a[1 + direction] * inv
    return rows


def adjoint_plane(c, lo, hi, w, clo, chi, halo_row, first, rows, lanes):
    rho, u1, u2, u3, pres, sponge, inv = [w(i) for i in range(7)]
    a = [c(f) for f in range(5)]
    al, ah = [lo(f) for f in range(5)], [hi(f) for f in range(5)]
    fl = flux(al, clo(0), clo(3), clo(1), clo(2), 0)
    fh = flux(ah, chi(0), chi(3), chi(1), chi(2), 0)
    fy = flux(a, rho, inv, u2, pres, 1)
    fz = flux(a, rho, inv, u3, pres, 2)
    out = []
    for f in range(5):
        r = halo_row(8 + f)
        yp, ym = shift_y(fy[f], jnp.where(first, 0.0, r), jnp.where(first, r, 0.0), rows)
        zp, zm = shift_z(fz[f], lanes)
        o = 0.5 * ((fh[f] - fl[f]) + (yp - ym) + (zp - zm)) - sponge * a[f]
        if f > 0:
            r = halo_row(f)
            yp, ym = shift_y(a[f], jnp.where(first, 0.0, r), jnp.where(first, r, 0.0), rows)
            zp, zm = shift_z(a[f], lanes)
            o = o + viscosity * ((al[f] + ah[f]) + (yp + ym) + (zp + zm) - 6.0 * a[f])
        out.append(o)
    return out


def kernel(
    n, count, init, term, forcing, dens, vel, pres, spon,
    others, qn, an, ao,
    state, halo, row_out, row_in, coef, coef_halo, coef_send, work_f, f_send, work_init, final,
    send, recv,
):
    tm = lax.axis_index("tm")
    s = lax.axis_index("space")
    group, part, core = s // 4, (s // 2) % 2, s % 2
    other = 1 - part
    half = init.shape[3] // 2
    sibling = s + 1 - 2 * core
    partner = s + 2 - 4 * part
    groups = count // 4
    has_ext = jnp.logical_or(
        jnp.logical_and(core == 0, group > 0), jnp.logical_and(core == 1, group < groups - 1)
    )
    ext = (group + 2 * core - 1) * 4 + part * 2 + 1 - core
    after, before = lax.rem(tm + 1, n), lax.rem(tm + n - 1, n)
    mine = pl.ds(pl.multiple_of(part * half, 8), half)
    theirs = pl.ds(pl.multiple_of(other * half, 8), half)
    first = part == 0

    barrier = pltpu.get_barrier_semaphore()
    greet = [(tm, sibling), (tm, partner), (after, partner)]
    if n > 2:
        greet.append((before, partner))
    greet += [(lax.rem(tm + d, n), s) for d in range(1, n)]
    for who in greet:
        pl.semaphore_signal(barrier, inc=1, device_id=who, device_id_type=MESH)

    @pl.when(has_ext)
    def _():
        pl.semaphore_signal(barrier, inc=1, device_id=(tm, ext), device_id_type=MESH)

    coef_send[0] = dens[0, theirs, :]
    for d in range(3):
        coef_send[1 + d] = vel[d, 0, theirs, :]
    coef_send[4] = pres[0, theirs, :]
    coef_send[5] = spon[0, theirs, :]

    pl.semaphore_wait(barrier, len(greet) + has_ext.astype(jnp.int32))

    def copy(i, src, dst, who):
        return pltpu.make_async_remote_copy(
            src_ref=src, dst_ref=dst, send_sem=send.at[i], recv_sem=recv.at[i],
            device_id=who, device_id_type=MESH,
        )

    started, started_ext = [], []

    def go(i, src, dst, who):
        c = copy(i, src, dst, who)
        c.start()
        started.append(c)
        return c

    def go_ext(i, src, dst):
        c = copy(i, src, dst, (tm, ext))

        @pl.when(has_ext)
        def _():
            c.start()

        started_ext.append(c)
        return c

    def arrived_ext(c):
        @pl.when(has_ext)
        def _():
            c.wait_recv()

    r_init = go(R_INIT, init.at[0, :, 0, theirs, :], state.at[0, 0, part], (tm, partner))
    r_coef = go(R_COEF, coef_send.at[pl.ds(0, 6)], coef.at[part, pl.ds(0, 6)], (tm, partner))
    r_term = go(R_TERM, term.at[0, :, 0, theirs, :], state.at[1, 0, part], (tm, partner))
    slab_copies = [
        go(SLAB + 2 * (d - 1), init.at[0, :, 0], others.at[d - 1], (lax.rem(tm + d, n), s))
        for d in range(1, n)
    ]

    def force(offset, rows):
        factors = force_factors(tm, offset, n)
        return [
            sum(factors[2 * k + r] * forcing[k, r, f, 0, rows, :] for k in range(NFREQ) for r in range(2))
            for f in range(5)
        ]

    for offset in range(2):
        for f, value in enumerate(force(offset, theirs)):
            f_send[offset, f] = value
    r_f0 = go(R_F0, f_send.at[0], work_f.at[0, part], (tm, partner))
    r_f1 = go(R_F1, f_send.at[1], work_f.at[1, part], (tm, partner))

    state[0, 0, part] = init[0, :, 0, mine, :]
    state[1, 0, part] = term[0, :, 0, mine, :]
    coef[part, 0] = dens[0, mine, :]
    for d in range(3):
        coef[part, 1 + d] = vel[d, 0, mine, :]
    coef[part, 4] = pres[0, mine, :]
    coef[part, 5] = spon[0, mine, :]
    for offset in range(2):
        for f, value in enumerate(force(offset, mine)):
            work_f[offset, part, f] = value

    @pl.when(jnp.logical_not(has_ext))
    def _():
        zeros = jnp.zeros(halo.shape[3:], jnp.float32)
        for eq in range(2):
            for stage in range(4):
                halo[eq, stage, 2 * core] = zeros
        coef_halo[2 * core, pl.ds(0, 3)] = jnp.ones((3,) + coef_halo.shape[2:], jnp.float32)

    nrows, nlanes = half, init.shape[4]
    rows = lax.broadcasted_iota(jnp.int32, (nrows, nlanes), 0)
    lanes = lax.broadcasted_iota(jnp.int32, (nrows, nlanes), 1)

    def edge(ref):
        return jnp.where(first, ref[nrows - 1 :, :], ref[0:1, :])

    halos = {}

    def send_halo(eq, stage):
        base = HALO + 3 * (4 * eq + stage)
        y = state.at[eq, stage]
        sib = go(base, y, halo.at[eq, stage, pl.ds(core, 2)], (tm, sibling))
        out = go_ext(base + 1, y.at[core], halo.at[eq, stage, 2 * (1 - core)])
        for k in range(2):
            a = [edge(y.at[k, f]) for f in range(5)]
            for f in range(5):
                row_out[eq, stage, k, f : f + 1, :] = a[f]
            if eq == 1:
                rho, u2, pr, inv = [edge(coef.at[k, i]) for i in (0, 2, 4, 6)]
                for f, value in enumerate(flux(a, rho, inv, u2, pr, 1)):
                    row_out[eq, stage, k, 8 + f : 9 + f, :] = value
        row = go(base + 2, row_out.at[eq, stage], row_in.at[eq, stage], (tm, partner))
        halos[eq, stage] = (sib, out, row)

    def wait_halo(eq, stage):
        sib, out, row = halos[eq, stage]
        sib.wait_recv()
        row.wait_recv()
        arrived_ext(out)

    r_init.wait_recv()
    send_halo(0, 0)
    init_copies = [
        go(
            SLAB + 2 * (d - 1) + 1, state.at[0, 0, other], work_init.at[d - 1, other],
            (lax.rem(tm + d, n), s),
        )
        for d in range(1, n)
    ]
    r_coef.wait_recv()
    for k in range(2):
        for i, source in enumerate((0, 1, 4)):
            coef_send[6 + 3 * k + i] = coef[k, source]
        coef[k, 6] = 1.0 / coef[k, 0]
    c_sib = []
    for k in range(2):
        c_sib.append(
            go(
                SLAB + 2 * (n - 1) + k, coef_send.at[pl.ds(6 + 3 * k, 3)],
                coef_halo.at[core + k, pl.ds(0, 3)], (tm, sibling),
            )
        )
    c_ext = go_ext(
        C_EXT, coef_send.at[pl.ds(6 + 3 * core, 3)], coef_halo.at[2 * (1 - core), pl.ds(0, 3)]
    )
    r_term.wait_recv()
    send_halo(1, 0)

    def react(offset, k, f):
        value = react_factor(offset, n) * state[0, 0, k, f]
        for d in range(1, n):
            value = value + react_factor(offset + 2 * d, n) * work_init[d - 1, k, f]
        return value

    def run_stage(eq, stage):
        wait_halo(eq, stage)
        if stage < 2 and eq == 0:
            (r_f0, r_f1)[stage].wait_recv()
        if eq == 1 and stage == 0:
            for c in c_sib:
                c.wait_recv()
            arrived_ext(c_ext)
            for k in range(3):
                coef_halo[k, 3] = 1.0 / coef_halo[k, 0]
            for d in range(1, n):
                slab_copies[d - 1].wait_recv()
                init_copies[d - 1].wait_recv()
                work_init[d - 1, part] = others[d - 1, :, mine, :]
        step = (0.5 * time_step, 0.5 * time_step, time_step)
        for k in range(2):
            c = lambda f: state[eq, stage, k, f]
            lo = lambda f: halo[eq, stage, k, f]
            hi = lambda f: halo[eq, stage, k + 1, f]
            w = lambda i: coef[k, i]
            row = lambda i: row_in[eq, stage, k, i : i + 1, :]
            if eq == 0:
                out = forward_plane(c, lo, hi, w, row, first, rows, lanes)
            else:
                clo = lambda i: coef_halo[k, i]
                chi = lambda i: coef_halo[k + 1, i]
                out = adjoint_plane(c, lo, hi, w, clo, chi, row, first, rows, lanes)
            for f in range(5):
                if stage < 3:
                    if eq == 0:
                        rate = out[f] + work_f[min(stage, 1), k, f]
                    else:
                        rate = out[f] + react(2 - min(stage, 1), k, f)
                    state[eq, stage + 1, k, f] = state[eq, 0, k, f] + step[stage] * rate
                else:
                    mix = state[eq, 1, k, f] + 2.0 * state[eq, 2, k, f] + state[eq, 3, k, f]
                    final[eq, k, f] = (mix - state[eq, 0, k, f]) * (1.0 / 3.0) + (
                        time_step / 6.0
                    ) * out[f]

    last = []

    def send_final(eq):
        target, place = ((after, qn), (before, an))[eq]
        last.append(go(FINAL + 2 * eq, final.at[eq, other], place.at[:, mine, :], (target, partner)))
        last.append(go(FINAL + 2 * eq + 1, final.at[eq, part], place.at[:, mine, :], (target, s)))
        if eq == 1:
            last.append(go(FINAL + 4, final.at[1, other], ao.at[:, mine, :], (tm, partner)))
            ao[:, mine, :] = final[1, part]

    for stage in range(4):
        for eq in range(2):
            run_stage(eq, stage)
            if stage < 3:
                send_halo(eq, stage + 1)
            else:
                send_final(eq)

    for c in last:
        c.wait_recv()
    for c in started:
        c.wait_send()

    @pl.when(has_ext)
    def _():
        for c in started_ext:
            c.wait_send()


def exchange(n, count, *args):
    ny, nz = args[0].shape[3:]
    half = ny // 2
    f32 = jnp.float32
    plane = jax.ShapeDtypeStruct((5, ny, nz), f32)
    vmem = pl.BlockSpec(memory_space=pltpu.VMEM)
    sems = SLAB + 2 * (n - 1) + 2
    return pl.pallas_call(
        functools.partial(kernel, n, count),
        out_shape=[jax.ShapeDtypeStruct((n - 1, 5, ny, nz), f32), plane, plane, plane],
        in_specs=[vmem] * 7,
        out_specs=[vmem] * 4,
        scratch_shapes=[
            pltpu.VMEM((2, 4, 2, 5, half, nz), f32),
            pltpu.VMEM((2, 4, 3, 5, half, nz), f32),
            pltpu.VMEM((2, 4, 2, 16, nz), f32),
            pltpu.VMEM((2, 4, 2, 16, nz), f32),
            pltpu.VMEM((2, 7, half, nz), f32),
            pltpu.VMEM((3, 4, half, nz), f32),
            pltpu.VMEM((12, half, nz), f32),
            pltpu.VMEM((2, 2, 5, half, nz), f32),
            pltpu.VMEM((2, 5, half, nz), f32),
            pltpu.VMEM((n - 1, 2, 5, half, nz), f32),
            pltpu.VMEM((2, 2, 5, half, nz), f32),
            pltpu.SemaphoreType.DMA((sems,)),
            pltpu.SemaphoreType.DMA((sems,)),
        ],
        compiler_params=pltpu.CompilerParams(
            collective_id=0, has_side_effects=True, vmem_limit_bytes=40 * 1024 * 1024
        ),
    )(*args)


def per_device(n, count, initial, terminal, forcing, density, velocity, pressure, sponge):
    others, qn, an, ao = exchange(
        n, count, initial, terminal, forcing, density, velocity, pressure, sponge
    )
    tm = lax.axis_index("tm")
    states = [initial[0, :, 0]] + [others[d - 1] for d in range(1, n)]

    def factor(function, k, shift):
        return picked([function(theta(k, 2 * ((j + shift) % n), n)) for j in range(n)], tm)

    def amplitudes(fields, shifts):
        rows = []
        for k in range(NFREQ):
            cos = [factor(math.cos, k, shift) / n for shift in shifts]
            sin = [factor(math.sin, k, shift) / n for shift in shifts]
            rows.append(sum(c * v for c, v in zip(cos, fields)))
            rows.append(-sum(c * v for c, v in zip(sin, fields)))
        return jnp.stack(rows).reshape((NFREQ, 2) + fields[0].shape)

    def react(offset):
        return sum(react_factor(offset + 2 * d, n) * states[d] for d in range(n))

    response = amplitudes(states, [-d for d in range(n)])[:, :, :, None]
    factors = force_factors(tm, 0, n)
    force = sum(factors[2 * k + r] * forcing[k, r, :, 0] for k in range(NFREQ) for r in range(2))
    next_initial = qn + (time_step / 6.0) * force
    next_terminal = an + (time_step / 6.0) * react(2)
    adjoint = ao + (time_step / 6.0) * react(0)
    if n == 2:
        rows = initial.shape[3] // n
        own = lax.dynamic_slice_in_dim(adjoint, tm * rows, rows, axis=1)
        far = lax.dynamic_slice_in_dim(next_terminal, tm * rows, rows, axis=1)
        projection = amplitudes([own, far], [0, 1])[:, :, :, None]
    else:
        projection = amplitudes([adjoint], [0])[:, :, :, None]
        projection = lax.psum_scatter(projection, "tm", scatter_dimension=4, tiled=True)
    return (next_initial[None, :, None], next_terminal[None, :, None], response, projection)


def solution(mesh):
    return jax.shard_map(
        functools.partial(per_device, mesh.shape["tm"], mesh.shape["space"]),
        mesh=mesh,
        in_specs=(
            P("tm", None, "space", None, None),
            P("tm", None, "space", None, None),
            P(None, None, None, "space", None, None),
            P("space", None, None),
            P(None, "space", None, None),
            P("space", None, None),
            P("space", None, None),
        ),
        out_specs=(
            P("tm", None, "space", None, None),
            P("tm", None, "space", None, None),
            P(None, None, None, "space", None, None),
            P(None, None, None, "space", "tm", None),
        ),
        check_vma=False,
    )
```

```python
import functools
import math

import jax
import jax.numpy as jnp
from jax import lax
from jax.experimental import pallas as pl
from jax.experimental.pallas import tpu as pltpu
from jax.sharding import PartitionSpec as P

NFREQ = 2
viscosity = 0.05
time_step = 0.25
MESH = pl.DeviceIdType.MESH

def theta(k, half_count, slabs):
    turns = (k + 1) * half_count % (2 * slabs)
    return 2.0 * math.pi * turns / (2 * slabs)


def picked(values, index):
    out = jnp.float32(values[0])
    for j in range(1, len(values)):
        out = jnp.where(index == j, jnp.float32(values[j]), out)
    return out


def force_factors(slab, offset, n):
    rows = []
    for k in range(NFREQ):
        rows.append(picked([math.cos(theta(k, 2 * j + offset, n)) for j in range(n)], slab))
        rows.append(picked([-math.sin(theta(k, 2 * j + offset, n)) for j in range(n)], slab))
    return rows


def react_factor(half_gap, n):
    return 2.0 / n * sum(math.cos(theta(k, half_gap, n)) for k in range(NFREQ))


def shift_y(x, above, below, rows):
    n = x.shape[0]
    minus = jnp.where(rows == 0, above, pltpu.roll(x, 1, 0))
    plus = jnp.where(rows == n - 1, below, pltpu.roll(x, n - 1, 0))
    return plus, minus


def shift_z(x, lanes):
    n = x.shape[1]
    minus = jnp.where(lanes == 0, 0.0, pltpu.roll(x, 1, 1))
    plus = jnp.where(lanes == n - 1, 0.0, pltpu.roll(x, n - 1, 1))
    return plus, minus


def forward_plane(c, lo, hi, w, halo_row, first, rows, lanes):
    rho, u1, u2, u3, pres, sponge, inv = [w(i) for i in range(7)]
    out = [None] * 5
    for f in range(5):
        v, a, b = c(f), lo(f), hi(f)
        r = halo_row(f)
        yp, ym = shift_y(v, jnp.where(first, 0.0, r), jnp.where(first, r, 0.0), rows)
        zp, zm = shift_z(v, lanes)
        dx, dy, dz = 0.5 * (b - a), 0.5 * (yp - ym), 0.5 * (zp - zm)
        o = -(u1 * dx + u2 * dy + u3 * dz) - sponge * v
        if f > 0:
            o = o + viscosity * ((a + b) + (yp + ym) + (zp + zm) - 6.0 * v)
        if f == 1:
            div = dx
        elif f == 2:
            div = div + dy
        elif f == 3:
            div = div + dz
        elif f == 4:
            out[1] = out[1] - inv * dx
            out[2] = out[2] - inv * dy
            out[3] = out[3] - inv * dz
        out[f] = o
    out[0] = out[0] - rho * div
    out[4] = out[4] - pres * div
    return out


def flux(a, rho, inv, speed, pres, direction):
    rows = [speed * a[i] for i in range(5)]
    rows[1 + direction] = rows[1 + direction] + rho * a[0] + pres * a[4]
    rows[4] = rows[4] + a[1 + direction] * inv
    return rows


def adjoint_plane(c, lo, hi, w, clo, chi, halo_row, first, rows, lanes):
    rho, u1, u2, u3, pres, sponge, inv = [w(i) for i in range(7)]
    a = [c(f) for f in range(5)]
    al, ah = [lo(f) for f in range(5)], [hi(f) for f in range(5)]
    fl = flux(al, clo(0), clo(3), clo(1), clo(2), 0)
    fh = flux(ah, chi(0), chi(3), chi(1), chi(2), 0)
    fy = flux(a, rho, inv, u2, pres, 1)
    fz = flux(a, rho, inv, u3, pres, 2)
    out = []
    for f in range(5):
        r = halo_row(8 + f)
        yp, ym = shift_y(fy[f], jnp.where(first, 0.0, r), jnp.where(first, r, 0.0), rows)
        zp, zm = shift_z(fz[f], lanes)
        o = 0.5 * ((fh[f] - fl[f]) + (yp - ym) + (zp - zm)) - sponge * a[f]
        if f > 0:
            r = halo_row(f)
            yp, ym = shift_y(a[f], jnp.where(first, 0.0, r), jnp.where(first, r, 0.0), rows)
            zp, zm = shift_z(a[f], lanes)
            o = o + viscosity * ((al[f] + ah[f]) + (yp + ym) + (zp + zm) - 6.0 * a[f])
        out.append(o)
    return out


def kernel(
    n, count, sems, init, term, forcing_hbm, dens, vel, pres, spon,
    others, qn, an, ao,
    state, halo, row_out, row_in, coef, coef_halo, coef_send, work_f, f_send, work_init, final,
    forcing, send, recv, local,
):
    tm = lax.axis_index("tm")
    s = lax.axis_index("space")
    group, part, core = s // 4, (s // 2) % 2, s % 2
    other = 1 - part
    half = init.shape[3] // 2
    sibling = s + 1 - 2 * core
    partner = s + 2 - 4 * part
    groups = count // 4
    has_ext = jnp.logical_or(
        jnp.logical_and(core == 0, group > 0), jnp.logical_and(core == 1, group < groups - 1)
    )
    ext = (group + 2 * core - 1) * 4 + part * 2 + 1 - core
    after, before = lax.rem(tm + 1, n), lax.rem(tm + n - 1, n)
    mine = pl.ds(pl.multiple_of(part * half, 8), half)
    theirs = pl.ds(pl.multiple_of(other * half, 8), half)
    first = part == 0

    barrier = pltpu.get_barrier_semaphore()
    greet = [(tm, sibling), (tm, partner), (before, partner), (after, partner)]
    if n == 2:
        greet.pop()
    greet += [(lax.rem(tm + d, n), s) for d in range(1, n)]
    for who in greet:
        pl.semaphore_signal(barrier, inc=1, device_id=who, device_id_type=MESH)

    @pl.when(has_ext)
    def _():
        pl.semaphore_signal(barrier, inc=1, device_id=(tm, ext), device_id_type=MESH)

    fetches = []

    def fetch(src, dst):
        c = pltpu.make_async_copy(src, dst, local.at[len(fetches)])
        c.start()
        fetches.append(c)

    fetch(forcing_hbm, forcing)
    fetch(dens.at[:, mine, :], coef.at[part, pl.ds(0, 1)])
    fetch(vel.at[:, 0, mine, :], coef.at[part, pl.ds(1, 3)])
    fetch(pres.at[:, mine, :], coef.at[part, pl.ds(4, 1)])
    fetch(spon.at[:, mine, :], coef.at[part, pl.ds(5, 1)])
    fetch(init.at[0, :, 0, mine, :], work_init.at[n - 2, part])

    pl.semaphore_wait(barrier, len(greet) + has_ext.astype(jnp.int32))

    started, started_ext = [], []

    def make(src, dst, who, out=None, into=None):
        if out is None:
            out = into = len(started) + len(started_ext)
            assert out < sems - 2
        return pltpu.make_async_remote_copy(
            src_ref=src, dst_ref=dst, send_sem=send.at[out], recv_sem=recv.at[into],
            device_id=who, device_id_type=MESH,
        )

    def go(src, dst, who):
        c = make(src, dst, who)
        c.start()
        started.append(c)
        return c

    def go_ext(src, dst):
        c = make(src, dst, (tm, ext))

        @pl.when(has_ext)
        def _():
            c.start()

        started_ext.append(c)
        return c

    def arrived_ext(c):
        @pl.when(has_ext)
        def _():
            c.wait_recv()

    s_theirs = go(init.at[0, :, 0, theirs, :], others.at[0, :, theirs, :], (after, s))
    r_coef = [
        go(dens.at[:, theirs, :], coef.at[part, pl.ds(0, 1)], (tm, partner)),
        go(vel.at[:, 0, theirs, :], coef.at[part, pl.ds(1, 3)], (tm, partner)),
        go(pres.at[:, theirs, :], coef.at[part, pl.ds(4, 1)], (tm, partner)),
        go(spon.at[:, theirs, :], coef.at[part, pl.ds(5, 1)], (tm, partner)),
    ]
    s_mine = go(init.at[0, :, 0, mine, :], others.at[0, :, mine, :], (after, s))
    r_term = [
        go(term.at[0, :, 0, theirs, :], state.at[1, 0, part], (before, partner)),
        go(term.at[0, :, 0, mine, :], state.at[1, 0, part], (before, s)),
    ]
    slab_copies = [
        go(init.at[0, :, 0], others.at[d - 1], (lax.rem(tm + d, n), s)) for d in range(2, n)
    ]

    def force(offset, rows):
        factors = force_factors(before, offset, n)
        return [
            sum(factors[2 * k + r] * forcing[k, r, f, 0, rows, :] for k in range(NFREQ) for r in range(2))
            for f in range(5)
        ]

    fetches[0].wait()
    for f, value in enumerate(force(0, theirs)):
        f_send[0, f] = value
    r_f0 = go(f_send.at[0], work_f.at[0, part], (tm, partner))
    for f, value in enumerate(force(1, theirs)):
        f_send[1, f] = value
    s_theirs.wait_recv()
    r_init = go(others.at[0, :, theirs, :], state.at[0, 0, part], (tm, partner))
    r_f1 = go(f_send.at[1], work_f.at[1, part], (tm, partner))

    for offset in range(2):
        for f, value in enumerate(force(offset, mine)):
            work_f[offset, part, f] = value

    @pl.when(jnp.logical_not(has_ext))
    def _():
        zeros = jnp.zeros(halo.shape[3:], jnp.float32)
        for eq in range(2):
            for stage in range(4):
                halo[eq, stage, 2 * core] = zeros
        coef_halo[2 * core, pl.ds(0, 3)] = jnp.ones((3,) + coef_halo.shape[2:], jnp.float32)

    nrows, nlanes = half, init.shape[4]
    rows = lax.broadcasted_iota(jnp.int32, (nrows, nlanes), 0)
    lanes = lax.broadcasted_iota(jnp.int32, (nrows, nlanes), 1)

    def edge(ref):
        return jnp.where(first, ref[nrows - 1 :, :], ref[0:1, :])

    halos = {}

    def send_halo(eq, stage):
        y = state.at[eq, stage]
        sib = go(y, halo.at[eq, stage, pl.ds(core, 2)], (tm, sibling))
        out = go_ext(y.at[core], halo.at[eq, stage, 2 * (1 - core)])
        for k in range(2):
            a = [edge(y.at[k, f]) for f in range(5)]
            for f in range(5):
                row_out[eq, stage, k, f : f + 1, :] = a[f]
            if eq == 1:
                rho, u2, pr, inv = [edge(coef.at[k, i]) for i in (0, 2, 4, 6)]
                for f, value in enumerate(flux(a, rho, inv, u2, pr, 1)):
                    row_out[eq, stage, k, 8 + f : 9 + f, :] = value
        row = go(row_out.at[eq, stage], row_in.at[eq, stage], (tm, partner))
        halos[eq, stage] = (sib, out, row)

    def wait_halo(eq, stage):
        sib, out, row = halos[eq, stage]
        sib.wait_recv()
        row.wait_recv()
        arrived_ext(out)

    for c in fetches[1:]:
        c.wait()
    for c in r_coef:
        c.wait_recv()
    for k in range(2):
        for i, source in enumerate((0, 1, 4)):
            coef_send[3 * k + i] = coef[k, source]
        coef[k, 6] = 1.0 / coef[k, 0]
    c_sib = [
        go(coef_send.at[pl.ds(3 * k, 3)], coef_halo.at[core + k, pl.ds(0, 3)], (tm, sibling))
        for k in range(2)
    ]
    c_ext = go_ext(coef_send.at[pl.ds(3 * core, 3)], coef_halo.at[2 * (1 - core), pl.ds(0, 3)])
    s_mine.wait_recv()
    state[0, 0, part] = others[0, :, mine, :]
    r_init.wait_recv()
    send_halo(0, 0)
    init_copies = [
        go(state.at[0, 0, other], work_init.at[d - 1, other], (lax.rem(tm + d, n), s))
        for d in range(1, n)
    ]
    for c in r_term:
        c.wait_recv()
    send_halo(1, 0)

    def react(offset, k, f):
        value = react_factor(offset + 4, n) * state[0, 0, k, f]
        for d in range(1, n):
            value = value + react_factor(offset + 4 + 2 * d, n) * work_init[d - 1, k, f]
        return value

    def run_stage(eq, stage):
        wait_halo(eq, stage)
        if stage < 2 and eq == 0:
            (r_f0, r_f1)[stage].wait_recv()
        if eq == 1 and stage == 0:
            for c in c_sib:
                c.wait_recv()
            arrived_ext(c_ext)
            for k in range(3):
                coef_halo[k, 3] = 1.0 / coef_halo[k, 0]
            for d in range(1, n):
                init_copies[d - 1].wait_recv()
            for d in range(2, n):
                slab_copies[d - 2].wait_recv()
                work_init[d - 2, part] = others[d - 1, :, mine, :]
        step = (0.5 * time_step, 0.5 * time_step, time_step)
        for k in range(2):
            c = lambda f: state[eq, stage, k, f]
            lo = lambda f: halo[eq, stage, k, f]
            hi = lambda f: halo[eq, stage, k + 1, f]
            w = lambda i: coef[k, i]
            row = lambda i: row_in[eq, stage, k, i : i + 1, :]
            if eq == 0:
                out = forward_plane(c, lo, hi, w, row, first, rows, lanes)
            else:
                clo = lambda i: coef_halo[k, i]
                chi = lambda i: coef_halo[k + 1, i]
                out = adjoint_plane(c, lo, hi, w, clo, chi, row, first, rows, lanes)
            for f in range(5):
                if stage < 3:
                    if eq == 0:
                        rate = out[f] + work_f[min(stage, 1), k, f]
                    else:
                        rate = out[f] + react(2 - min(stage, 1), k, f)
                    state[eq, stage + 1, k, f] = state[eq, 0, k, f] + step[stage] * rate
                else:
                    mix = state[eq, 1, k, f] + 2.0 * state[eq, 2, k, f] + state[eq, 3, k, f]
                    final[eq, k, f] = (mix - state[eq, 0, k, f]) * (1.0 / 3.0) + (
                        time_step / 6.0
                    ) * out[f]

    last = []

    def send_final(eq):
        place = (qn, an)[eq]
        last.append(go(final.at[eq, other], place.at[:, mine, :], (tm, partner)))
        if eq == 1 and n == 2:
            to_same = make(final.at[eq, part], ao, (after, s), sems - 1, sems - 1)
            to_cross = make(final.at[eq, other], ao, (after, partner), sems - 2, sems - 1)

            @pl.when(part == after)
            def _():
                to_same.start()
                to_cross.start()

            last.append(to_same)
            ends.append((to_same, to_cross))
        place[:, mine, :] = final[eq, part]

    ends = []
    for stage in range(4):
        for eq in (0, 1) if stage < 3 else (1, 0):
            run_stage(eq, stage)
            if stage < 3:
                send_halo(eq, stage + 1)
            else:
                send_final(eq)

    for c in last:
        c.wait_recv()
    for c in started:
        c.wait_send()
    for to_same, to_cross in ends:

        @pl.when(part == after)
        def _():
            to_same.wait_send()
            to_cross.wait_send()

    @pl.when(has_ext)
    def _():
        for c in started_ext:
            c.wait_send()


def exchange(n, count, *args):
    ny, nz = args[0].shape[3:]
    half = ny // 2
    f32 = jnp.float32
    plane = jax.ShapeDtypeStruct((5, ny, nz), f32)
    chunk = jax.ShapeDtypeStruct((5, ny // n, nz), f32)
    vmem = pl.BlockSpec(memory_space=pltpu.VMEM)
    sems = 48 + 2 * n
    hbm = pl.BlockSpec(memory_space=pltpu.HBM)
    return pl.pallas_call(
        functools.partial(kernel, n, count, sems),
        out_shape=[jax.ShapeDtypeStruct((n - 1, 5, ny, nz), f32), plane, plane, chunk],
        in_specs=[hbm] * 7,
        out_specs=[vmem] * 4,
        scratch_shapes=[
            pltpu.VMEM((2, 4, 2, 5, half, nz), f32),
            pltpu.VMEM((2, 4, 3, 5, half, nz), f32),
            pltpu.VMEM((2, 4, 2, 16, nz), f32),
            pltpu.VMEM((2, 4, 2, 16, nz), f32),
            pltpu.VMEM((2, 7, half, nz), f32),
            pltpu.VMEM((3, 4, half, nz), f32),
            pltpu.VMEM((6, half, nz), f32),
            pltpu.VMEM((2, 2, 5, half, nz), f32),
            pltpu.VMEM((2, 5, half, nz), f32),
            pltpu.VMEM((n - 1, 2, 5, half, nz), f32),
            pltpu.VMEM((2, 2, 5, half, nz), f32),
            pltpu.VMEM(args[2].shape, f32),
            pltpu.SemaphoreType.DMA((sems,)),
            pltpu.SemaphoreType.DMA((sems,)),
            pltpu.SemaphoreType.DMA((6,)),
        ],
        compiler_params=pltpu.CompilerParams(
            collective_id=0, has_side_effects=True, vmem_limit_bytes=40 * 1024 * 1024
        ),
    )(*args)


def per_device(n, count, initial, terminal, forcing, density, velocity, pressure, sponge):
    others, qn, an, ao = exchange(
        n, count, initial, terminal, forcing, density, velocity, pressure, sponge
    )
    tm = lax.axis_index("tm")
    states = [initial[0, :, 0]] + [others[d - 1] for d in range(1, n)]

    def factor(function, k, shift):
        return picked([function(theta(k, 2 * ((j + shift) % n), n)) for j in range(n)], tm)

    def amplitudes(fields, shifts):
        rows = []
        for k in range(NFREQ):
            cos = [factor(math.cos, k, shift) / n for shift in shifts]
            sin = [factor(math.sin, k, shift) / n for shift in shifts]
            rows.append(sum(c * v for c, v in zip(cos, fields)))
            rows.append(-sum(c * v for c, v in zip(sin, fields)))
        return jnp.stack(rows).reshape((NFREQ, 2) + fields[0].shape)

    def react(offset):
        return sum(react_factor(offset + 2 * d, n) * states[d] for d in range(n))

    response = amplitudes(states, [-d for d in range(n)])[:, :, :, None]
    factors = force_factors(tm, 0, n)
    force = sum(factors[2 * k + r] * forcing[k, r, :, 0] for k in range(NFREQ) for r in range(2))
    next_initial = qn + (time_step / 6.0) * force
    next_terminal = an + (time_step / 6.0) * react(2)
    if n == 2:
        rows = initial.shape[3] // n
        chunk = lambda v: lax.dynamic_slice_in_dim(v, tm * rows, rows, axis=1)
        own = ao + (time_step / 6.0) * chunk(react(0))
        projection = amplitudes([own, chunk(next_terminal)], [0, 1])[:, :, :, None]
    else:
        projection = amplitudes([next_terminal], [1])[:, :, :, None]
        projection = lax.psum_scatter(projection, "tm", scatter_dimension=4, tiled=True)
    return (next_initial[None, :, None], next_terminal[None, :, None], response, projection)


def solution(mesh):
    return jax.shard_map(
        functools.partial(per_device, mesh.shape["tm"], mesh.shape["space"]),
        mesh=mesh,
        in_specs=(
            P("tm", None, "space", None, None),
            P("tm", None, "space", None, None),
            P(None, None, None, "space", None, None),
            P("space", None, None),
            P(None, "space", None, None),
            P("space", None, None),
            P("space", None, None),
        ),
        out_specs=(
            P("tm", None, "space", None, None),
            P("tm", None, "space", None, None),
            P(None, None, None, "space", None, None),
            P(None, None, None, "space", "tm", None),
        ),
        check_vma=False,
    )
```

```python
import functools
import math

import jax
import jax.numpy as jnp
from jax import lax
from jax.experimental import pallas as pl
from jax.experimental.pallas import tpu as pltpu
from jax.sharding import PartitionSpec as P

NFREQ = 2
viscosity = 0.05
time_step = 0.25
ORDER = ((1, 0), (0, 0), (1, 1), (0, 1), (1, 2), (0, 2), (1, 3), (0, 3))
MESH = pl.DeviceIdType.MESH

def theta(k, half_count, slabs):
    turns = (k + 1) * half_count % (2 * slabs)
    return 2.0 * math.pi * turns / (2 * slabs)


def picked(values, index):
    out = jnp.float32(values[0])
    for j in range(1, len(values)):
        out = jnp.where(index == j, jnp.float32(values[j]), out)
    return out


def force_factors(slab, offset, n):
    rows = []
    for k in range(NFREQ):
        rows.append(picked([math.cos(theta(k, 2 * j + offset, n)) for j in range(n)], slab))
        rows.append(picked([-math.sin(theta(k, 2 * j + offset, n)) for j in range(n)], slab))
    return rows


def react_factor(half_gap, n):
    return 2.0 / n * sum(math.cos(theta(k, half_gap, n)) for k in range(NFREQ))


def shift_y(x, above, below, rows):
    n = x.shape[0]
    minus = jnp.where(rows == 0, above, pltpu.roll(x, 1, 0))
    plus = jnp.where(rows == n - 1, below, pltpu.roll(x, n - 1, 0))
    return plus, minus


def shift_z(x, lanes):
    n = x.shape[1]
    minus = jnp.where(lanes == 0, 0.0, pltpu.roll(x, 1, 1))
    plus = jnp.where(lanes == n - 1, 0.0, pltpu.roll(x, n - 1, 1))
    return plus, minus


def forward_plane(c, lo, hi, w, halo_row, first, rows, lanes):
    rho, u1, u2, u3, pres, sponge, inv = [w(i) for i in range(7)]
    out = [None] * 5
    for f in range(5):
        v, a, b = c(f), lo(f), hi(f)
        r = halo_row(f)
        yp, ym = shift_y(v, jnp.where(first, 0.0, r), jnp.where(first, r, 0.0), rows)
        zp, zm = shift_z(v, lanes)
        dx, dy, dz = 0.5 * (b - a), 0.5 * (yp - ym), 0.5 * (zp - zm)
        o = -(u1 * dx + u2 * dy + u3 * dz) - sponge * v
        if f > 0:
            o = o + viscosity * ((a + b) + (yp + ym) + (zp + zm) - 6.0 * v)
        if f == 1:
            div = dx
        elif f == 2:
            div = div + dy
        elif f == 3:
            div = div + dz
        elif f == 4:
            out[1] = out[1] - inv * dx
            out[2] = out[2] - inv * dy
            out[3] = out[3] - inv * dz
        out[f] = o
    out[0] = out[0] - rho * div
    out[4] = out[4] - pres * div
    return out


def flux(a, rho, inv, speed, pres, direction):
    rows = [speed * a[i] for i in range(5)]
    rows[1 + direction] = rows[1 + direction] + rho * a[0] + pres * a[4]
    rows[4] = rows[4] + a[1 + direction] * inv
    return rows


def adjoint_plane(c, lo, hi, w, clo, chi, halo_row, first, rows, lanes):
    rho, u1, u2, u3, pres, sponge, inv = [w(i) for i in range(7)]
    a = [c(f) for f in range(5)]
    al, ah = [lo(f) for f in range(5)], [hi(f) for f in range(5)]
    fl = flux(al, clo(0), clo(3), clo(1), clo(2), 0)
    fh = flux(ah, chi(0), chi(3), chi(1), chi(2), 0)
    fy = flux(a, rho, inv, u2, pres, 1)
    fz = flux(a, rho, inv, u3, pres, 2)
    out = []
    for f in range(5):
        r = halo_row(8 + f)
        yp, ym = shift_y(fy[f], jnp.where(first, 0.0, r), jnp.where(first, r, 0.0), rows)
        zp, zm = shift_z(fz[f], lanes)
        o = 0.5 * ((fh[f] - fl[f]) + (yp - ym) + (zp - zm)) - sponge * a[f]
        if f > 0:
            r = halo_row(f)
            yp, ym = shift_y(a[f], jnp.where(first, 0.0, r), jnp.where(first, r, 0.0), rows)
            zp, zm = shift_z(a[f], lanes)
            o = o + viscosity * ((al[f] + ah[f]) + (yp + ym) + (zp + zm) - 6.0 * a[f])
        out.append(o)
    return out


def kernel(
    n, count, sems, init, term, forcing_hbm, dens, vel, pres, spon,
    others, qn, an, ao,
    state, halo, row_out, row_in, coef, coef_halo, coef_send, work_f, f_send, work_init, final,
    forcing, send, recv, local,
):
    tm = lax.axis_index("tm")
    s = lax.axis_index("space")
    group, part, core = s // 4, (s // 2) % 2, s % 2
    other = 1 - part
    half = init.shape[3] // 2
    sibling = s + 1 - 2 * core
    partner = s + 2 - 4 * part
    groups = count // 4
    has_ext = jnp.logical_or(
        jnp.logical_and(core == 0, group > 0), jnp.logical_and(core == 1, group < groups - 1)
    )
    ext = (group + 2 * core - 1) * 4 + part * 2 + 1 - core
    after, before = lax.rem(tm + 1, n), lax.rem(tm + n - 1, n)
    mine = pl.ds(pl.multiple_of(part * half, 8), half)
    theirs = pl.ds(pl.multiple_of(other * half, 8), half)
    first = part == 0

    barrier = pltpu.get_barrier_semaphore()
    greet = [(tm, sibling), (tm, partner), (before, partner), (after, partner)]
    if n == 2:
        greet.pop()
    greet += [(lax.rem(tm + d, n), s) for d in range(1, n)]
    for who in greet:
        pl.semaphore_signal(barrier, inc=1, device_id=who, device_id_type=MESH)

    @pl.when(has_ext)
    def _():
        pl.semaphore_signal(barrier, inc=1, device_id=(tm, ext), device_id_type=MESH)

    fetches = []

    def fetch(src, dst):
        c = pltpu.make_async_copy(src, dst, local.at[len(fetches)])
        c.start()
        fetches.append(c)

    fetch(forcing_hbm, forcing)
    fetch(dens.at[:, mine, :], coef.at[part, pl.ds(0, 1)])
    fetch(vel.at[:, 0, mine, :], coef.at[part, pl.ds(1, 3)])
    fetch(pres.at[:, mine, :], coef.at[part, pl.ds(4, 1)])
    fetch(spon.at[:, mine, :], coef.at[part, pl.ds(5, 1)])
    fetch(init.at[0, :, 0, mine, :], work_init.at[n - 2, part])
    fetch(term.at[0, :, 0, mine, :], state.at[1, 0, part])

    pl.semaphore_wait(barrier, len(greet) + has_ext.astype(jnp.int32))

    started, started_ext = [], []

    def make(src, dst, who, out=None, into=None):
        if out is None:
            out = into = len(started) + len(started_ext)
            assert out < sems - 2
        return pltpu.make_async_remote_copy(
            src_ref=src, dst_ref=dst, send_sem=send.at[out], recv_sem=recv.at[into],
            device_id=who, device_id_type=MESH,
        )

    def go(src, dst, who):
        c = make(src, dst, who)
        c.start()
        started.append(c)
        return c

    def go_ext(src, dst):
        c = make(src, dst, (tm, ext))

        @pl.when(has_ext)
        def _():
            c.start()

        started_ext.append(c)
        return c

    def arrived_ext(c):
        @pl.when(has_ext)
        def _():
            c.wait_recv()

    s_theirs = go(init.at[0, :, 0, theirs, :], others.at[0, :, theirs, :], (after, s))
    r_term = go(term.at[0, :, 0, theirs, :], state.at[1, 0, part], (tm, partner))
    r_coef = [
        go(dens.at[:, theirs, :], coef.at[part, pl.ds(0, 1)], (tm, partner)),
        go(vel.at[:, 0, theirs, :], coef.at[part, pl.ds(1, 3)], (tm, partner)),
        go(pres.at[:, theirs, :], coef.at[part, pl.ds(4, 1)], (tm, partner)),
        go(spon.at[:, theirs, :], coef.at[part, pl.ds(5, 1)], (tm, partner)),
    ]
    s_mine = go(init.at[0, :, 0, mine, :], others.at[0, :, mine, :], (after, s))
    slab_copies = [
        go(init.at[0, :, 0], others.at[d - 1], (lax.rem(tm + d, n), s)) for d in range(2, n)
    ]

    def force(offset, rows):
        factors = force_factors(before, offset, n)
        return [
            sum(factors[2 * k + r] * forcing[k, r, f, 0, rows, :] for k in range(NFREQ) for r in range(2))
            for f in range(5)
        ]

    fetches[0].wait()
    for f, value in enumerate(force(0, theirs)):
        f_send[0, f] = value
    s_theirs.wait_recv()
    r_init = go(others.at[0, :, theirs, :], state.at[0, 0, part], (tm, partner))
    r_f0 = go(f_send.at[0], work_f.at[0, part], (tm, partner))
    for f, value in enumerate(force(1, theirs)):
        f_send[1, f] = value

    for offset in range(2):
        for f, value in enumerate(force(offset, mine)):
            work_f[offset, part, f] = value

    @pl.when(jnp.logical_not(has_ext))
    def _():
        zeros = jnp.zeros(halo.shape[3:], jnp.float32)
        for eq in range(2):
            for stage in range(4):
                halo[eq, stage, 2 * core] = zeros
        coef_halo[2 * core, pl.ds(0, 3)] = jnp.ones((3,) + coef_halo.shape[2:], jnp.float32)

    nrows, nlanes = half, init.shape[4]
    rows = lax.broadcasted_iota(jnp.int32, (nrows, nlanes), 0)
    lanes = lax.broadcasted_iota(jnp.int32, (nrows, nlanes), 1)

    def edge(ref):
        return jnp.where(first, ref[nrows - 1 :, :], ref[0:1, :])

    halos = {}

    def send_halo(eq, stage):
        y = state.at[eq, stage]
        sib = go(y, halo.at[eq, stage, pl.ds(core, 2)], (tm, sibling))
        out = go_ext(y.at[core], halo.at[eq, stage, 2 * (1 - core)])
        for k in range(2):
            a = [edge(y.at[k, f]) for f in range(5)]
            for f in range(5):
                row_out[eq, stage, k, f : f + 1, :] = a[f]
            if eq == 1:
                rho, u2, pr, inv = [edge(coef.at[k, i]) for i in (0, 2, 4, 6)]
                for f, value in enumerate(flux(a, rho, inv, u2, pr, 1)):
                    row_out[eq, stage, k, 8 + f : 9 + f, :] = value
        row = go(row_out.at[eq, stage], row_in.at[eq, stage], (tm, partner))
        halos[eq, stage] = (sib, out, row)

    def wait_halo(eq, stage):
        sib, out, row = halos[eq, stage]
        sib.wait_recv()
        row.wait_recv()
        arrived_ext(out)

    for c in fetches[1:]:
        c.wait()
    for c in r_coef:
        c.wait_recv()
    for k in range(2):
        for i, source in enumerate((0, 1, 4)):
            coef_send[3 * k + i] = coef[k, source]
        coef[k, 6] = 1.0 / coef[k, 0]
    c_sib = [
        go(coef_send.at[pl.ds(3 * k, 3)], coef_halo.at[core + k, pl.ds(0, 3)], (tm, sibling))
        for k in range(2)
    ]
    c_ext = go_ext(coef_send.at[pl.ds(3 * core, 3)], coef_halo.at[2 * (1 - core), pl.ds(0, 3)])
    r_term.wait_recv()
    send_halo(1, 0)
    s_mine.wait_recv()
    state[0, 0, part] = others[0, :, mine, :]
    r_init.wait_recv()
    send_halo(0, 0)
    init_copies = [
        go(state.at[0, 0, other], work_init.at[d - 1, other], (lax.rem(tm + d, n), s))
        for d in range(1, n)
    ]
    r_f1 = go(f_send.at[1], work_f.at[1, part], (tm, partner))

    def react(offset, k, f):
        value = react_factor(offset + 2, n) * state[0, 0, k, f]
        for d in range(1, n):
            value = value + react_factor(offset + 2 + 2 * d, n) * work_init[d - 1, k, f]
        return value

    def run_stage(eq, stage):
        wait_halo(eq, stage)
        if stage < 2 and eq == 0:
            (r_f0, r_f1)[stage].wait_recv()
        if eq == 1 and stage == 0:
            for c in c_sib:
                c.wait_recv()
            arrived_ext(c_ext)
            for k in range(3):
                coef_halo[k, 3] = 1.0 / coef_halo[k, 0]
            for d in range(1, n):
                init_copies[d - 1].wait_recv()
            for d in range(2, n):
                slab_copies[d - 2].wait_recv()
                work_init[d - 2, part] = others[d - 1, :, mine, :]
        step = (0.5 * time_step, 0.5 * time_step, time_step)
        for k in range(2):
            c = lambda f: state[eq, stage, k, f]
            lo = lambda f: halo[eq, stage, k, f]
            hi = lambda f: halo[eq, stage, k + 1, f]
            w = lambda i: coef[k, i]
            row = lambda i: row_in[eq, stage, k, i : i + 1, :]
            if eq == 0:
                out = forward_plane(c, lo, hi, w, row, first, rows, lanes)
            else:
                clo = lambda i: coef_halo[k, i]
                chi = lambda i: coef_halo[k + 1, i]
                out = adjoint_plane(c, lo, hi, w, clo, chi, row, first, rows, lanes)
            for f in range(5):
                if stage < 3:
                    if eq == 0:
                        rate = out[f] + work_f[min(stage, 1), k, f]
                    else:
                        rate = out[f] + react(2 - min(stage, 1), k, f)
                    state[eq, stage + 1, k, f] = state[eq, 0, k, f] + step[stage] * rate
                else:
                    mix = state[eq, 1, k, f] + 2.0 * state[eq, 2, k, f] + state[eq, 3, k, f]
                    final[eq, k, f] = (mix - state[eq, 0, k, f]) * (1.0 / 3.0) + (
                        time_step / 6.0
                    ) * out[f]

    last = []

    def send_final(eq):
        if eq == 0:
            last.append(go(final.at[0, other], qn.at[:, mine, :], (tm, partner)))
            qn[:, mine, :] = final[0, part]
            return
        last.append(go(final.at[1, other], an.at[:, mine, :], (before, partner)))
        last.append(go(final.at[1, part], an.at[:, mine, :], (before, s)))
        if n == 2:
            c = make(final.at[1, other], ao, (tm, partner), sems - 1, sems - 1)

            @pl.when(part == tm)
            def _():
                c.start()
                ao[...] = final[1, part]

            ends.append(c)

    ends = []
    for eq, stage in ORDER:
        run_stage(eq, stage)
        if stage < 3:
            send_halo(eq, stage + 1)
        else:
            send_final(eq)

    for c in last:
        c.wait_recv()
    for c in started:
        c.wait_send()
    for c in ends:

        @pl.when(part == tm)
        def _():
            c.wait_send()

        @pl.when(part != tm)
        def _():
            c.wait_recv()

    @pl.when(has_ext)
    def _():
        for c in started_ext:
            c.wait_send()


def exchange(n, count, *args):
    ny, nz = args[0].shape[3:]
    half = ny // 2
    f32 = jnp.float32
    plane = jax.ShapeDtypeStruct((5, ny, nz), f32)
    chunk = jax.ShapeDtypeStruct((5, ny // n, nz), f32)
    vmem = pl.BlockSpec(memory_space=pltpu.VMEM)
    sems = 48 + 2 * n
    hbm = pl.BlockSpec(memory_space=pltpu.HBM)
    return pl.pallas_call(
        functools.partial(kernel, n, count, sems),
        out_shape=[jax.ShapeDtypeStruct((n - 1, 5, ny, nz), f32), plane, plane, chunk],
        in_specs=[hbm] * 7,
        out_specs=[vmem] * 4,
        scratch_shapes=[
            pltpu.VMEM((2, 4, 2, 5, half, nz), f32),
            pltpu.VMEM((2, 4, 3, 5, half, nz), f32),
            pltpu.VMEM((2, 4, 2, 16, nz), f32),
            pltpu.VMEM((2, 4, 2, 16, nz), f32),
            pltpu.VMEM((2, 7, half, nz), f32),
            pltpu.VMEM((3, 4, half, nz), f32),
            pltpu.VMEM((6, half, nz), f32),
            pltpu.VMEM((2, 2, 5, half, nz), f32),
            pltpu.VMEM((2, 5, half, nz), f32),
            pltpu.VMEM((n - 1, 2, 5, half, nz), f32),
            pltpu.VMEM((2, 2, 5, half, nz), f32),
            pltpu.VMEM(args[2].shape, f32),
            pltpu.SemaphoreType.DMA((sems,)),
            pltpu.SemaphoreType.DMA((sems,)),
            pltpu.SemaphoreType.DMA((7,)),
        ],
        compiler_params=pltpu.CompilerParams(
            collective_id=0, has_side_effects=True, vmem_limit_bytes=60 * 1024 * 1024
        ),
    )(*args)


def per_device(n, count, initial, terminal, forcing, density, velocity, pressure, sponge):
    others, qn, an, ao = exchange(
        n, count, initial, terminal, forcing, density, velocity, pressure, sponge
    )
    tm = lax.axis_index("tm")
    states = [initial[0, :, 0]] + [others[d - 1] for d in range(1, n)]

    def factor(function, k, shift):
        return picked([function(theta(k, 2 * ((j + shift) % n), n)) for j in range(n)], tm)

    def amplitudes(fields, shifts):
        rows = []
        for k in range(NFREQ):
            cos = [factor(math.cos, k, shift) / n for shift in shifts]
            sin = [factor(math.sin, k, shift) / n for shift in shifts]
            rows.append(sum(c * v for c, v in zip(cos, fields)))
            rows.append(-sum(c * v for c, v in zip(sin, fields)))
        return jnp.stack(rows).reshape((NFREQ, 2) + fields[0].shape)

    def react(offset):
        return sum(react_factor(offset + 2 * d, n) * states[d] for d in range(n))

    response = amplitudes(states, [-d for d in range(n)])[:, :, :, None]
    factors = force_factors(tm, 0, n)
    force = sum(factors[2 * k + r] * forcing[k, r, :, 0] for k in range(NFREQ) for r in range(2))
    next_initial = qn + (time_step / 6.0) * force
    next_terminal = an + (time_step / 6.0) * react(2)
    if n == 2:
        rows = initial.shape[3] // n
        chunk = lambda v: lax.dynamic_slice_in_dim(v, tm * rows, rows, axis=1)
        own = ao + (time_step / 6.0) * chunk(react(0))
        projection = amplitudes([own, chunk(next_terminal)], [0, 1])[:, :, :, None]
    else:
        projection = amplitudes([next_terminal], [1])[:, :, :, None]
        projection = lax.psum_scatter(projection, "tm", scatter_dimension=4, tiled=True)
    return (next_initial[None, :, None], next_terminal[None, :, None], response, projection)


def solution(mesh):
    return jax.shard_map(
        functools.partial(per_device, mesh.shape["tm"], mesh.shape["space"]),
        mesh=mesh,
        in_specs=(
            P("tm", None, "space", None, None),
            P("tm", None, "space", None, None),
            P(None, None, None, "space", None, None),
            P("space", None, None),
            P(None, "space", None, None),
            P("space", None, None),
            P("space", None, None),
        ),
        out_specs=(
            P("tm", None, "space", None, None),
            P("tm", None, "space", None, None),
            P(None, None, None, "space", None, None),
            P(None, None, None, "space", "tm", None),
        ),
        check_vma=False,
    )
```
